512 devices in a mesh: ctx: 32 (over z, y_hi, core), tp: 16 (over x, y_lo).
Axes of the slice: x: 4, y: 8 (y_hi: 2, y_lo: 4; y = y_hi * 4 + y_lo), z: 8, core: 2. Of those that a mesh axis runs over, the one named last changes fastest.
Arguments:
- queries: bfloat16 [4096, 32, 128], P('ctx', 'tp'), may hold values from -6 to 6
- incoming_keys: bfloat16 [4096, 4, 128], P('ctx'), may hold values from -6 to 6
- incoming_values: bfloat16 [4096, 4, 128], P('ctx'), may hold values from -6 to 6
- cache_keys: bfloat16 [8192, 4, 128], P('ctx'), may hold values from -6 to 6
- stored_value_rows: bfloat16 [8192, 4, 128], P('ctx'), may hold values from -6 to 6
- cache_valid: int32 [32], P('ctx'), may hold values from 1 to 256, 4096 in all
- out_weight: bfloat16 [4096, 8192], P('tp'), may hold values from -3 to 3
Outputs:
- projected: bfloat16 [4096, 8192], P('ctx', 'tp')
The draws below stay inside these ranges and needn't reach their ends.
Inputs may be any that keep to these rules, and one draw needn't show every extreme that they name: `cache_valid`: each cache block has at least one live slot.
All inputs are finite; a program needn't handle non-finite values.
Results may differ from the reference program's by a relative error of at most 0.024.
Values may be sent and summed in bfloat16 or wider, within the bound.
A program may use at most 64 MiB of HBM per device.

```python
import math
import jax
import jax.numpy as jnp
import numpy as np
from jax import lax

D = 8192
QUERY_HEADS = 32
KEY_VALUE_HEADS = 4
HEAD_DIMENSION = 128
CACHE_DEV = 256
BLOCKS = 32
NEW_TOKEN_TOTAL = 4096
CACHE_SLOT_TOTAL = 8192
N_TP = 16


def draw_queries(key, part):
    key = jax.random.fold_in(key, 11)
    value_tensor = jnp.clip(jax.random.normal(key, (NEW_TOKEN_TOTAL, QUERY_HEADS, HEAD_DIMENSION), jnp.float32), -4.0, 4.0)
    return value_tensor.astype(jnp.bfloat16)


def draw_cache_keys(key, part):
    key = jax.random.fold_in(key, 23)
    value_tensor = jnp.clip(1.5 * jax.random.normal(key, (CACHE_SLOT_TOTAL, KEY_VALUE_HEADS, HEAD_DIMENSION), jnp.float32), -6.0, 6.0)
    return value_tensor.astype(jnp.bfloat16)


def steps_of(key, dims, cuts, smallest, high):
    level, own = 1.0, jax.random.fold_in(key, 6)
    for axis_at, blocks in cuts:
        heights = jnp.exp(jax.random.uniform(jax.random.fold_in(own, axis_at), (blocks,), jnp.float32, smallest / len(cuts), high / len(cuts)))
        level = level * jnp.repeat(heights, dims[axis_at] // blocks).reshape([-1 if axis == axis_at else 1 for axis in range(len(dims))])
    return level


def length_profile(number_of, total, reach, skew):
    portions = [(1 << 20) // math.isqrt(grade ** skew) + 1 for grade in range(2, number_of + 1)]
    spare, holding = total - reach - (number_of - 1), [1] * (number_of - 1)
    while spare > 0:
        candidates = [i for i in range(number_of - 1) if holding[i] < reach]
        whole, left = sum([portions[i] for i in candidates]), spare
        for i in candidates:
            addition = min(reach - holding[i], max(1, left * portions[i] // whole), spare)
            holding[i] = holding[i] + addition
            spare = spare - addition
    return np.array([reach] + holding)


def uneven(key, number_of, total, reach, lean):
    if number_of == 2:
        one = jax.random.randint(key, (), max(1, total - reach), min(reach, total - 1) + 1)
        return jnp.stack([one, total - one])
    tallies = jnp.asarray(length_profile(number_of, total, reach, lean), jnp.int32)
    couples = (number_of - 1) // 2
    giver, sink = tallies[1:1 + 2 * couples:2], tallies[2:2 + 2 * couples:2]
    margin = jnp.minimum(giver - 1, reach - sink)
    moved = jax.random.randint(jax.random.fold_in(key, 1), (couples,), 0, 1 << 20) % (margin + 1)
    tallies = tallies.at[1:1 + 2 * couples:2].set(giver - moved).at[2:2 + 2 * couples:2].set(sink + moved)
    return tallies[jax.random.permutation(jax.random.fold_in(key, 2), number_of)]


def gaussian(own_key, extent, deviation, most, pieces=(), kind=jnp.bfloat16):
    gain = steps_of(own_key, extent, pieces, -0.22, 0.18) if pieces else 1.0
    entries = jax.random.normal(own_key, extent, jnp.float32) * deviation * gain
    return jnp.minimum(jnp.maximum(entries, -most), most).astype(kind)


def setup_inputs(seed: int = 0) -> dict:
    streams_of = jax.random.split(jax.random.key(seed), 8)
    return {
        "queries": draw_queries(jax.random.fold_in(streams_of[7], 71), 0),
        "incoming_keys": gaussian(streams_of[1], (NEW_TOKEN_TOTAL, KEY_VALUE_HEADS, HEAD_DIMENSION), 1.5, 6.0, ((0, 32),)),
        "incoming_values": gaussian(streams_of[2], (NEW_TOKEN_TOTAL, KEY_VALUE_HEADS, HEAD_DIMENSION), 1.0, 6.0, ((0, 32),)),
        "cache_keys": draw_cache_keys(jax.random.fold_in(streams_of[7], 71), 0),
        "stored_value_rows": gaussian(streams_of[4], (CACHE_SLOT_TOTAL, KEY_VALUE_HEADS, HEAD_DIMENSION), 1.0, 6.0, ((0, 32),)),
        "cache_valid": uneven(streams_of[5], BLOCKS, CACHE_DEV * BLOCKS // 2, CACHE_DEV, 2).astype(jnp.int32),
        "out_weight": gaussian(streams_of[6], (QUERY_HEADS * HEAD_DIMENSION, D), 0.5, 3.0, ((0, 16),)),
    }


masked_score = -1e30
far_position = 2 ** 30


def reference(queries, incoming_keys, incoming_values, cache_keys, stored_value_rows, cache_valid, out_weight):
    group_width = QUERY_HEADS // KEY_VALUE_HEADS
    scale_factor = HEAD_DIMENSION ** -0.5
    cache_rows = jnp.arange(CACHE_SLOT_TOTAL, dtype=jnp.int32)
    live_slot = (cache_rows % CACHE_DEV) < cache_valid[cache_rows // CACHE_DEV]
    cache_pos = jnp.where(live_slot, -1, far_position).astype(jnp.int32)
    key_pos = jnp.concatenate([cache_pos, jnp.arange(NEW_TOKEN_TOTAL, dtype=jnp.int32)])
    block_len = math.gcd(NEW_TOKEN_TOTAL, 512)
    block_count = NEW_TOKEN_TOTAL // block_len
    starts = (jnp.arange(block_count, dtype=jnp.int32) * block_len).astype(jnp.int32)
    per_group = []
    for key_value_head in range(KEY_VALUE_HEADS):
        key_rows = jnp.concatenate([cache_keys[:, key_value_head, :], incoming_keys[:, key_value_head, :]], axis=0)
        value_rows = jnp.concatenate([stored_value_rows[:, key_value_head, :], incoming_values[:, key_value_head, :]], axis=0)
        query_group = queries[:, key_value_head * group_width:(key_value_head + 1) * group_width, :]
        query_blocks = query_group.reshape(block_count, block_len * group_width, HEAD_DIMENSION)

        def attend(inputs):
            query_block, first_pos = inputs
            scores = jnp.dot(query_block, key_rows.T, preferred_element_type=jnp.float32) * scale_factor
            query_pos = first_pos + jnp.arange(block_len * group_width, dtype=jnp.int32) // group_width
            scores = jnp.where(key_pos[None, :] <= query_pos[:, None], scores, masked_score)
            row_max = jnp.max(scores, axis=1)
            weights = jnp.exp(scores - row_max[:, None])
            row_sum = jnp.sum(weights, axis=1)
            weighted = jnp.dot(weights.astype(jnp.bfloat16), value_rows, preferred_element_type=jnp.float32)
            return (weighted / row_sum[:, None]).astype(jnp.bfloat16)

        result = lax.map(attend, (query_blocks, starts))
        per_group.append(result.reshape(NEW_TOKEN_TOTAL, group_width, HEAD_DIMENSION))
    attended = jnp.concatenate(per_group, axis=1).reshape(NEW_TOKEN_TOTAL, QUERY_HEADS * HEAD_DIMENSION)
    span = (QUERY_HEADS // N_TP) * HEAD_DIMENSION
    summed = jnp.zeros((NEW_TOKEN_TOTAL, D), jnp.float32)
    for group_index in range(N_TP):
        partial_term = jnp.dot(attended[:, group_index * span:(group_index + 1) * span],
                               out_weight[group_index * span:(group_index + 1) * span, :],
                               preferred_element_type=jnp.float32).astype(jnp.bfloat16)
        partial_term = lax.optimization_barrier(partial_term)
        summed = summed + partial_term.astype(jnp.float32)
    return summed.astype(jnp.bfloat16)
```

```python
import functools

import jax
import jax.numpy as jnp
from jax import lax
from jax.experimental import pallas as pl
from jax.experimental.pallas import tpu as pltpu
from jax.sharding import PartitionSpec as P

MESH = pl.DeviceIdType.MESH
F32 = jnp.float32
BF16 = jnp.bfloat16

NX = 4
NY = 4
NZ = 8
NS = 4
HEAD = 128
TOK = 128
CACHE = 256
CQ = CACHE // NY
TQ = TOK // NY
KEYS = CQ + TQ
META = 2 * KEYS
ROWS = META + 16
FEAT = 512
SPAN = NY * FEAT
MASKED = -1e30
SCALE = HEAD ** (-0.5) * 1.4426950408889634


def nt(a, b):
    return lax.dot_general(a, b, (((1,), (1,)), ((), ())), preferred_element_type=F32)


def tn(a, b):
    return lax.dot_general(a, b, (((0,), (0,)), ((), ())), preferred_element_type=F32)


def pick(rows, wide, step, first):
    r = lax.broadcasted_iota(jnp.int32, (rows, wide), 0)
    c = lax.broadcasted_iota(jnp.int32, (rows, wide), 1)
    return jnp.where(c == step * r + first, 1.0, 0.0).astype(BF16)


def kernel(
    valid_ref, q_hbm, ik_hbm, iv_hbm, ck_hbm, cv_hbm, w_hbm, out_ref,
    q_raw, ck_raw, cv_raw, ik_raw, iv_raw,
    q_all, kv, bias, m_ref, l_ref, acc,
    o_send, o_recv, lse_send, lse_recv,
    att, wall, r_send, r_recv, own_out,
    local_sem, q_ss, q_rs, kv_ss, kv_rs, sib_ss, sib_rs, o_ss, o_rs, e_ss, e_rs,
    w_ss, w_rs, ws_ss, ws_rs, a_ss, a_rs, r_ss, r_rs,
):
    ctx = lax.axis_index("ctx")
    tp = lax.axis_index("tp")
    x, y = tp // NY, tp % NY
    z, shard = ctx // NS, ctx % NS
    y_hi, core = shard // 2, shard % 2
    quarter = y_hi * (NY - 1 - y) + (1 - y_hi) * y
    up = (lax.rem(z + 1, NZ) * NS + shard, tp)
    down = (lax.rem(z + NZ - 1, NZ) * NS + shard, tp)
    sibling = (z * NS + y_hi * 2 + (1 - core), tp)
    mirror = (z * NS + (1 - y_hi) * 2 + core, x * NY + (NY - 1 - y))
    y_at = [lax.rem(y + d, NY) for d in range(NY)]
    x_at = [lax.rem(x + d, NX) for d in range(NX)]
    y_peer = [(ctx, x * NY + y_at[d]) for d in range(NY)]
    x_peer = [(ctx, x_at[d] * NY + y) for d in range(NX)]

    def send(src, dst, ss, rs, to):
        copy = pltpu.make_async_remote_copy(
            src_ref=src, dst_ref=dst, send_sem=ss, recv_sem=rs, device_id=to, device_id_type=MESH
        )
        copy.start()
        return copy

    def fetch(src, dst, sem):
        copy = pltpu.make_async_copy(src, dst, sem)
        copy.start()
        return copy

    sent = []

    c_at = pl.multiple_of(quarter * (CQ * NX), CQ * NX)
    t_at = pl.multiple_of(quarter * (TQ * NX), TQ * NX)
    loads = [
        fetch(ck_hbm.at[pl.ds(c_at, CQ * NX)], ck_raw, local_sem.at[0]),
        fetch(ik_hbm.at[pl.ds(t_at, TQ * NX)], ik_raw, local_sem.at[1]),
        fetch(cv_hbm.at[pl.ds(c_at, CQ * NX)], cv_raw, local_sem.at[2]),
        fetch(iv_hbm.at[pl.ds(t_at, TQ * NX)], iv_raw, local_sem.at[3]),
        fetch(q_hbm, q_raw, local_sem.at[4]),
    ]

    barrier = pltpu.get_barrier_semaphore()
    partners = [up, down, sibling, mirror] + y_peer[1:] + x_peer[1:]
    for partner in partners:
        pl.semaphore_signal(barrier, inc=1, device_id=partner, device_id_type=MESH)

    take_c = pick(CQ, CQ * NX, NX, x)
    take_t = pick(TQ, TQ * NX, NX, x)
    own = kv.at[z, shard]
    own[META:ROWS] = jnp.full((16, HEAD), valid_ref[0].astype(F32), F32).astype(BF16)
    loads[0].wait()
    own[0:CQ] = jnp.dot(take_c, ck_raw[...], preferred_element_type=F32).astype(BF16)
    loads[1].wait()
    own[CQ:KEYS] = jnp.dot(take_t, ik_raw[...], preferred_element_type=F32).astype(BF16)
    loads[2].wait()
    own[KEYS:KEYS + CQ] = jnp.dot(take_c, cv_raw[...], preferred_element_type=F32).astype(BF16)
    loads[3].wait()
    own[KEYS + CQ:META] = jnp.dot(take_t, iv_raw[...], preferred_element_type=F32).astype(BF16)
    loads[4].wait()
    for h in range(2):
        q_all[y, h * TOK:(h + 1) * TOK] = jnp.dot(
            pick(TOK, 2 * TOK, 2, h), q_raw[...], preferred_element_type=F32
        ).astype(BF16)

    pl.semaphore_wait(barrier, len(partners))

    types = [shard, (1 - y_hi) * 2 + core]
    sib_types = [y_hi * 2 + (1 - core), (1 - y_hi) * 2 + (1 - core)]

    def slot(k):
        return lax.rem(z + k + NZ, NZ)

    def ring(way, kind, step):
        at = kv.at[slot(-step if way == 0 else step), types[kind]]
        sent.append(
            send(at, at, kv_ss.at[way, kind, step], kv_rs.at[way, kind, step], up if way == 0 else down)
        )

    def to_sibling(kind, k, index):
        at = kv.at[slot(k), types[kind]]
        sent.append(send(at, at, sib_ss.at[kind, index], sib_rs.at[kind, index], sibling))

    def arrived(ref, sem):
        pltpu.make_async_copy(ref, ref, sem).wait()

    mirrored = send(own, own, kv_ss.at[0, 0, 4], kv_rs.at[0, 0, 4], mirror)
    sent.append(mirrored)
    ring(0, 0, 0)
    ring(1, 0, 0)
    to_sibling(0, 0, 0)
    q_own = q_all.at[y]
    for d in (2, 1, 3):
        sent.append(send(q_own, q_own, q_ss.at[d], q_rs.at[d], y_peer[d]))

    half = pl.ds(pl.multiple_of(core * TOK, TOK), TOK)
    for d in (2, 1, 3):
        sent.append(
            send(
                w_hbm.at[half, pl.ds(pl.multiple_of(x_at[d] * SPAN, SPAN), SPAN)],
                wall.at[x, half],
                w_ss.at[d],
                w_rs.at[d],
                x_peer[d],
            )
        )
    w_own = fetch(
        w_hbm.at[:, pl.ds(pl.multiple_of(x * SPAN, SPAN), SPAN)], wall.at[x], local_sem.at[5]
    )

    token = lax.broadcasted_iota(jnp.int32, (TQ, HEAD), 1) + ctx * TOK
    new_at = lax.broadcasted_iota(jnp.int32, (TQ, HEAD), 0) + quarter * TQ
    slot_at = (lax.broadcasted_iota(jnp.int32, (CQ, HEAD), 0) + quarter * CQ).astype(F32)

    def absorb(zs, first):
        for s in range(NS):
            live = kv[zs, s, META:META + 1, :].astype(F32)
            bias[s * KEYS:s * KEYS + CQ] = jnp.where(slot_at < live, 0.0, MASKED)
            bias[s * KEYS + CQ:(s + 1) * KEYS] = jnp.where(
                new_at + (zs * NS + s) * TOK <= token, 0.0, MASKED
            )

        def step(j, carry):
            keys = jnp.concatenate([kv[zs, s, 0:KEYS] for s in range(NS)], axis=0)
            values = jnp.concatenate([kv[zs, s, KEYS:META] for s in range(NS)], axis=0)
            b = bias[...]
            scores = nt(keys, q_all[j]) * SCALE + jnp.concatenate([b, b], axis=1)
            top = jnp.max(scores, axis=0, keepdims=True)
            if first:
                weights = jnp.exp2(scores - top)
                m_ref[j] = top
                l_ref[j] = jnp.sum(weights, axis=0, keepdims=True)
                acc[j] = tn(values, weights.astype(BF16))
            else:
                old = m_ref[j]
                new = jnp.maximum(old, top)
                rescale = jnp.exp2(old - new)
                weights = jnp.exp2(scores - new)
                m_ref[j] = new
                l_ref[j] = l_ref[j] * rescale + jnp.sum(weights, axis=0, keepdims=True)
                acc[j] = acc[j] * rescale + tn(values, weights.astype(BF16))
            return carry

        lax.fori_loop(0, NY, step, 0)

    arrived(kv.at[z, types[1]], kv_rs.at[0, 0, 4])
    ring(0, 1, 0)
    ring(1, 1, 0)
    to_sibling(1, 0, 0)
    for d in (1, 2, 3):
        arrived(q_all.at[y_at[d]], q_rs.at[NY - d])
    for kind in range(2):
        arrived(kv.at[z, sib_types[kind]], sib_rs.at[kind, 0])
    absorb(z, True)

    for k in range(1, 4):
        for kind in range(2):
            arrived(kv.at[slot(-k), types[kind]], kv_rs.at[0, kind, k - 1])
            if k < 3 or kind == 0:
                ring(0, kind, k)
            to_sibling(kind, -k, 2 * k - 1)
            arrived(kv.at[slot(k), types[kind]], kv_rs.at[1, kind, k - 1])
            if k < 3 or kind == 1:
                ring(1, kind, k)
            to_sibling(kind, k, 2 * k)
        for kind in range(2):
            arrived(kv.at[slot(-k), sib_types[kind]], sib_rs.at[kind, 2 * k - 1])
        absorb(slot(-k), False)
        for kind in range(2):
            arrived(kv.at[slot(k), sib_types[kind]], sib_rs.at[kind, 2 * k])
        absorb(slot(k), False)
    for kind in range(2):
        arrived(kv.at[slot(4), types[kind]], kv_rs.at[kind, kind, 3])
        to_sibling(kind, 4, 7)
    for kind in range(2):
        arrived(kv.at[slot(4), sib_types[kind]], sib_rs.at[kind, 7])
    absorb(slot(4), False)

    for d in (2, 1, 3, 0):
        j = y_at[d]
        total = l_ref[j]
        o_send[d] = (acc[j] / total).astype(BF16)
        lse_send[d] = jnp.broadcast_to(m_ref[j] + jnp.log2(total), (8, 2 * TOK))
        if d:
            sent.append(send(o_send.at[d], o_recv.at[d], o_ss.at[d], o_rs.at[d], y_peer[d]))
            sent.append(send(lse_send.at[d], lse_recv.at[d], e_ss.at[d], e_rs.at[d], y_peer[d]))
    for d in (1, 2, 3):
        arrived(o_recv.at[d], o_rs.at[d])
        arrived(lse_recv.at[d], e_rs.at[d])
    lse = [lse_send[0][0:1]] + [lse_recv[d][0:1] for d in (1, 2, 3)]
    top = jnp.maximum(jnp.maximum(lse[0], lse[1]), jnp.maximum(lse[2], lse[3]))
    share = [jnp.exp2(e - top) for e in lse]
    whole = share[0] + share[1] + share[2] + share[3]
    mixed = o_send[0].astype(F32) * (share[0] / whole)
    for d in (1, 2, 3):
        mixed = mixed + o_recv[d].astype(F32) * (share[d] / whole)
    for h in range(2):
        att[x, :, h * HEAD:(h + 1) * HEAD] = mixed[:, h * TOK:(h + 1) * TOK].T.astype(BF16)
    a_own = att.at[x]
    for d in (2, 1, 3):
        sent.append(send(a_own, a_own, a_ss.at[d], a_rs.at[d], x_peer[d]))

    for d in (1, 2, 3):
        at = wall.at[x_at[d], half]
        arrived(at, w_rs.at[NX - d])
        sent.append(send(at, at, ws_ss.at[d], ws_rs.at[d], sibling))
    w_own.wait()
    other = pl.ds(pl.multiple_of((1 - core) * TOK, TOK), TOK)
    for d in (1, 2, 3):
        arrived(att.at[x_at[d]], a_rs.at[NX - d])
        arrived(wall.at[x_at[d], other], ws_rs.at[d])

    for d in (2, 1, 3, 0):
        cols = pl.ds(pl.multiple_of(y_at[d] * FEAT, FEAT), FEAT)
        part = jnp.dot(att[0], wall[0, :, cols], preferred_element_type=F32)
        for i in range(1, NX):
            part = part + jnp.dot(att[i], wall[i, :, cols], preferred_element_type=F32)
        if d:
            r_send[d] = part.astype(BF16)
            sent.append(send(r_send.at[d], r_recv.at[d], r_ss.at[d], r_rs.at[d], y_peer[d]))
        else:
            own_out[...] = part
    for d in (1, 2, 3):
        arrived(r_recv.at[d], r_rs.at[d])
    out_ref[...] = (
        own_out[...] + r_recv[1].astype(F32) + r_recv[2].astype(F32) + r_recv[3].astype(F32)
    ).astype(BF16)
    for copy in sent:
        copy.wait_send()


def local(
    queries, incoming_keys, incoming_values, cache_keys, stored_value_rows, cache_valid, out_weight
):
    flat = [
        a.reshape(a.shape[0] * a.shape[1], a.shape[2])
        for a in (queries, incoming_keys, incoming_values, cache_keys, stored_value_rows)
    ]
    hbm = pl.BlockSpec(memory_space=pltpu.HBM)
    vmem = pltpu.VMEM
    dma = pltpu.SemaphoreType.DMA
    return pl.pallas_call(
        kernel,
        name="attend_project",
        out_shape=jax.ShapeDtypeStruct((TOK, FEAT), BF16),
        in_specs=[pl.BlockSpec(memory_space=pltpu.SMEM)] + [hbm] * 6,
        out_specs=pl.BlockSpec(memory_space=pltpu.VMEM),
        scratch_shapes=[
            vmem((2 * TOK, HEAD), BF16),
            vmem((CQ * NX, HEAD), BF16),
            vmem((CQ * NX, HEAD), BF16),
            vmem((TQ * NX, HEAD), BF16),
            vmem((TQ * NX, HEAD), BF16),
            vmem((NY, 2 * TOK, HEAD), BF16),
            vmem((NZ, NS, ROWS, HEAD), BF16),
            vmem((NS * KEYS, HEAD), F32),
            vmem((NY, 1, 2 * TOK), F32),
            vmem((NY, 1, 2 * TOK), F32),
            vmem((NY, HEAD, 2 * TOK), F32),
            vmem((NY, HEAD, 2 * TOK), BF16),
            vmem((NY, HEAD, 2 * TOK), BF16),
            vmem((NY, 8, 2 * TOK), F32),
            vmem((NY, 8, 2 * TOK), F32),
            vmem((NX, TOK, 2 * HEAD), BF16),
            vmem((NX, 2 * HEAD, SPAN), BF16),
            vmem((NY, TOK, FEAT), BF16),
            vmem((NY, TOK, FEAT), BF16),
            vmem((TOK, FEAT), F32),
            dma((6,)),
            dma((4,)), dma((4,)),
            dma((2, 2, 5)), dma((2, 2, 5)),
            dma((2, 8)), dma((2, 8)),
            dma((4,)), dma((4,)),
            dma((4,)), dma((4,)),
            dma((4,)), dma((4,)),
            dma((4,)), dma((4,)),
            dma((4,)), dma((4,)),
            dma((4,)), dma((4,)),
        ],
        compiler_params=pltpu.CompilerParams(
            collective_id=0, has_side_effects=True, vmem_limit_bytes=40 * 2**20
        ),
        cost_estimate=pl.CostEstimate(
            flops=2_200_000_000, bytes_accessed=6_000_000, transcendentals=3_200_000
        ),
    )(cache_valid, *flat, out_weight)


def solution(mesh):
    placed = (
        P("ctx", "tp", None),
        P("ctx", None, None),
        P("ctx", None, None),
        P("ctx", None, None),
        P("ctx", None, None),
        P("ctx"),
        P("tp", None),
    )
    return jax.shard_map(
        local, mesh=mesh, in_specs=placed, out_specs=P("ctx", "tp"), check_vma=False
    )
```

```python
import jax
import jax.numpy as jnp
from jax import lax
from jax.experimental import pallas as pl
from jax.experimental.pallas import tpu as pltpu
from jax.sharding import PartitionSpec as P

MESH = pl.DeviceIdType.MESH
F32 = jnp.float32
BF16 = jnp.bfloat16

NX = 4
NY = 4
NZ = 8
NS = 4
HEAD = 128
TOK = 128
HALF = TOK // 2
CACHE = 256
CQ = CACHE // NY
TQ = TOK // NY
KEYS = CQ + TQ
META = 2 * KEYS
ROWS = META + 16
FEAT = 512
SPAN = NY * FEAT
MASKED = -1e30
VMEM_LIMIT = 64 * 2**20
SCALE = HEAD ** (-0.5) * 1.4426950408889634


def nt(a, b):
    return lax.dot_general(a, b, (((1,), (1,)), ((), ())), preferred_element_type=F32)


def tn(a, b):
    return lax.dot_general(a, b, (((0,), (0,)), ((), ())), preferred_element_type=F32)


def pick(rows, wide, step, first):
    r = lax.broadcasted_iota(jnp.int32, (rows, wide), 0)
    c = lax.broadcasted_iota(jnp.int32, (rows, wide), 1)
    return jnp.where(c == step * r + first, 1.0, 0.0).astype(BF16)


def kernel(
    valid_ref, q_hbm, ik_hbm, iv_hbm, ck_hbm, cv_hbm, w_hbm, out_ref,
    q_raw, ck_raw, cv_raw, ik_raw, iv_raw,
    q_all, kv, bias, m_ref, l_ref, acc,
    o_send, o_recv,
    att, wall, r_send, r_recv, far_out, own_out,
    local_sem, q_ss, q_rs, kv_ss, kv_rs, sib_ss, sib_rs, o_ss, o_rs,
    w_ss, w_rs, ws_ss, ws_rs, a_ss, a_rs, r_ss, r_rs,
):
    ctx = lax.axis_index("ctx")
    tp = lax.axis_index("tp")
    x, y = tp // NY, tp % NY
    z, shard = ctx // NS, ctx % NS
    y_hi, core = shard // 2, shard % 2
    quarter = y_hi * (NY - 1 - y) + (1 - y_hi) * y
    up = (lax.rem(z + 1, NZ) * NS + shard, tp)
    down = (lax.rem(z + NZ - 1, NZ) * NS + shard, tp)
    sibling = (z * NS + y_hi * 2 + (1 - core), tp)
    mirror = (z * NS + (1 - y_hi) * 2 + core, x * NY + (NY - 1 - y))
    y_at = [lax.rem(y + d, NY) for d in range(NY)]
    x_at = [lax.rem(x + d, NX) for d in range(NX)]
    y_peer = [(ctx, x * NY + y_at[d]) for d in range(NY)]
    x_peer = [(ctx, x_at[d] * NY + y) for d in range(NX)]

    def send(src, dst, ss, rs, to):
        copy = pltpu.make_async_remote_copy(
            src_ref=src, dst_ref=dst, send_sem=ss, recv_sem=rs, device_id=to, device_id_type=MESH
        )
        copy.start()
        return copy

    def fetch(src, dst, sem):
        copy = pltpu.make_async_copy(src, dst, sem)
        copy.start()
        return copy

    sent = []

    barrier = pltpu.get_barrier_semaphore()
    partners = [up, down, sibling, mirror] + y_peer[1:] + x_peer[1:]
    for partner in partners:
        pl.semaphore_signal(barrier, inc=1, device_id=partner, device_id_type=MESH)

    c_at = pl.multiple_of(quarter * (CQ * NX), CQ * NX)
    t_at = pl.multiple_of(quarter * (TQ * NX), TQ * NX)
    loads = [
        fetch(ck_hbm.at[pl.ds(c_at, CQ * NX)], ck_raw, local_sem.at[0]),
        fetch(ik_hbm.at[pl.ds(t_at, TQ * NX)], ik_raw, local_sem.at[1]),
        fetch(cv_hbm.at[pl.ds(c_at, CQ * NX)], cv_raw, local_sem.at[2]),
        fetch(iv_hbm.at[pl.ds(t_at, TQ * NX)], iv_raw, local_sem.at[3]),
        fetch(q_hbm, q_raw, local_sem.at[4]),
    ]

    take_c = pick(CQ, CQ * NX, NX, x)
    take_t = pick(TQ, TQ * NX, NX, x)
    own = kv.at[z, shard]
    own[META:ROWS] = jnp.full((16, HEAD), valid_ref[0].astype(F32), F32).astype(BF16)
    loads[0].wait()
    own[0:CQ] = jnp.dot(take_c, ck_raw[...], preferred_element_type=F32).astype(BF16)
    loads[1].wait()
    own[CQ:KEYS] = jnp.dot(take_t, ik_raw[...], preferred_element_type=F32).astype(BF16)
    loads[2].wait()
    own[KEYS:KEYS + CQ] = jnp.dot(take_c, cv_raw[...], preferred_element_type=F32).astype(BF16)
    loads[3].wait()
    own[KEYS + CQ:META] = jnp.dot(take_t, iv_raw[...], preferred_element_type=F32).astype(BF16)
    loads[4].wait()
    for i in range(4):
        q_all[0, i * HALF:(i + 1) * HALF] = jnp.dot(
            pick(HALF, 2 * TOK, 2, (i // 2) * TOK + i % 2), q_raw[...], preferred_element_type=F32
        ).astype(BF16)

    pl.semaphore_wait(barrier, len(partners))

    types = [shard, (1 - y_hi) * 2 + core]
    sib_types = [y_hi * 2 + (1 - core), (1 - y_hi) * 2 + (1 - core)]

    def slot(k):
        return lax.rem(z + k + NZ, NZ)

    def arrived(ref, sem):
        pltpu.make_async_copy(ref, ref, sem).wait()

    def ring(way, kind, step):
        at = kv.at[slot(-step if way == 0 else step), types[kind]]
        sent.append(
            send(at, at, kv_ss.at[way, kind, step], kv_rs.at[way, kind, step], up if way == 0 else down)
        )

    def to_sibling(kind, k):
        at = kv.at[slot(k), types[kind]]
        i = k % NZ
        sent.append(send(at, at, sib_ss.at[kind, i], sib_rs.at[kind, i], sibling))

    def from_sibling(k):
        for kind in range(2):
            arrived(kv.at[slot(k), sib_types[kind]], sib_rs.at[kind, k % NZ])

    def pass_on(kind, k):
        if k < 4 or kind == 0:
            arrived(kv.at[slot(-k), types[kind]], kv_rs.at[0, kind, k - 1])
            if k < 3 or (k == 3 and kind == 0):
                ring(0, kind, k)
            to_sibling(kind, -k)
        if k < 4 or kind == 1:
            arrived(kv.at[slot(k), types[kind]], kv_rs.at[1, kind, k - 1])
            if k < 3 or (k == 3 and kind == 1):
                ring(1, kind, k)
            to_sibling(kind, k)

    sent.append(send(own, own, kv_ss.at[0, 0, 4], kv_rs.at[0, 0, 4], mirror))
    ring(0, 0, 0)
    ring(1, 0, 0)
    to_sibling(0, 0)
    for d in (2, 1, 3):
        sent.append(send(q_all.at[0], q_all.at[NY - d], q_ss.at[d], q_rs.at[NY - d], y_peer[d]))

    half = pl.ds(pl.multiple_of(core * TOK, TOK), TOK)
    for d in (2, 1, 3):
        sent.append(
            send(
                w_hbm.at[half, pl.ds(pl.multiple_of(x_at[d] * SPAN, SPAN), SPAN)],
                wall.at[x, half],
                w_ss.at[d],
                w_rs.at[d],
                x_peer[d],
            )
        )
    w_own = fetch(
        w_hbm.at[:, pl.ds(pl.multiple_of(x * SPAN, SPAN), SPAN)], wall.at[x], local_sem.at[5]
    )

    lane = lax.broadcasted_iota(jnp.int32, (TQ, 2 * TOK), 1)
    token = lane // TOK * HALF + lane % HALF + ctx * TOK
    new_at = lax.broadcasted_iota(jnp.int32, (TQ, 2 * TOK), 0) + quarter * TQ
    slot_at = (lax.broadcasted_iota(jnp.int32, (CQ, HEAD), 0) + quarter * CQ).astype(F32)

    def absorb(k, rows=range(NY), first=False, masks=True):
        zs = slot(k)
        if masks:
            for s in range(NS):
                live = kv[zs, s, META:META + 1, :].astype(F32)
                b = jnp.where(slot_at < live, 0.0, MASKED)
                bias[s * KEYS:s * KEYS + CQ] = jnp.concatenate([b, b], axis=1)
                bias[s * KEYS + CQ:(s + 1) * KEYS] = jnp.where(
                    new_at + (zs * NS + s) * TOK <= token, 0.0, MASKED
                )
        keys = jnp.concatenate([kv[zs, s, 0:KEYS] for s in range(NS)], axis=0)
        values = jnp.concatenate([kv[zs, s, KEYS:META] for s in range(NS)], axis=0)

        def scored(j):
            return nt(keys, q_all[j]) * SCALE + bias[...]

        ready = scored(rows[0])
        for j in rows:
            scores = ready
            if j != rows[-1]:
                ready = scored(j + 1)
            top = jnp.max(scores, axis=0, keepdims=True)
            if first:
                weights = jnp.exp2(scores - top)
                m_ref[j] = top
                l_ref[j] = jnp.sum(weights, axis=0, keepdims=True)
                acc[j] = tn(values, weights.astype(BF16))
            else:
                old = m_ref[j]
                new = jnp.maximum(old, top)
                rescale = jnp.exp2(old - new)
                weights = jnp.exp2(scores - new)
                m_ref[j] = new
                l_ref[j] = l_ref[j] * rescale + jnp.sum(weights, axis=0, keepdims=True)
                acc[j] = acc[j] * rescale + tn(values, weights.astype(BF16))

    arrived(kv.at[z, types[1]], kv_rs.at[0, 0, 4])
    ring(0, 1, 0)
    ring(1, 1, 0)
    to_sibling(1, 0)
    pass_on(0, 1)
    from_sibling(0)
    absorb(0, range(1), first=True)
    pass_on(1, 1)
    for d in (1, 2, 3):
        arrived(q_all.at[d], q_rs.at[d])
    absorb(0, range(1, NY), first=True, masks=False)
    for k in range(2, 4):
        pass_on(0, k)
        from_sibling(1 - k)
        absorb(1 - k)
        pass_on(1, k)
        from_sibling(k - 1)
        absorb(k - 1)
    pass_on(0, 4)
    from_sibling(-3)
    absorb(-3)
    pass_on(1, 4)
    from_sibling(3)
    absorb(3)
    from_sibling(4)
    absorb(4)

    def parts(e):
        row = lax.broadcasted_iota(jnp.int32, (16, TOK), 0)
        high = e.astype(BF16).astype(F32)
        middle = (e - high).astype(BF16).astype(F32)
        return jnp.where(row == 0, high, jnp.where(row == 1, middle, e - high - middle)).astype(BF16)

    own_lse = [None, None]
    for h in range(2):
        lanes = slice(h * TOK, (h + 1) * TOK)
        for d in (2, 1, 3, 0):
            total = l_ref[d, :, lanes]
            o_send[h, d, 0:HEAD] = (acc[d, :, lanes] / total).astype(BF16)
            e = m_ref[d, :, lanes] + jnp.log2(total)
            if d:
                o_send[h, d, HEAD:] = parts(e)
                sent.append(send(o_send.at[h, d], o_recv.at[h, d], o_ss.at[h, d], o_rs.at[h, d], y_peer[d]))
            else:
                own_lse[h] = e
    for d in (1, 2, 3):
        at = wall.at[x_at[d], half]
        arrived(at, w_rs.at[NX - d])
        sent.append(send(at, at, ws_ss.at[d], ws_rs.at[d], sibling))
    for h in range(2):
        lse = [own_lse[h]]
        for d in (1, 2, 3):
            arrived(o_recv.at[h, d], o_rs.at[h, d])
            e = o_recv[h, d, HEAD:].astype(F32)
            lse.append(e[0:1] + e[1:2] + e[2:3])
        top = jnp.maximum(jnp.maximum(lse[0], lse[1]), jnp.maximum(lse[2], lse[3]))
        share = [jnp.exp2(e - top) for e in lse]
        whole = share[0] + share[1] + share[2] + share[3]
        mixed = o_send[h, 0, 0:HEAD].astype(F32) * (share[0] / whole)
        for d in (1, 2, 3):
            mixed = mixed + o_recv[h, d, 0:HEAD].astype(F32) * (share[d] / whole)
        turned = mixed.T.astype(BF16)
        att[h, x, :, 0:HEAD] = turned[0:HALF]
        att[h, x, :, HEAD:2 * HEAD] = turned[HALF:TOK]
        a_own = att.at[h, x]
        for d in (2, 1, 3):
            sent.append(send(a_own, a_own, a_ss.at[h, d], a_rs.at[h, d], x_peer[d]))
    w_own.wait()
    other = pl.ds(pl.multiple_of((1 - core) * TOK, TOK), TOK)

    at_end = jnp.logical_or(y == 0, y == NY - 1)
    near = y + 1 - 2 * lax.rem(y, 2)
    middle = jnp.where(y < 2, 2, 1)
    far = jnp.where(y < 2, 3, 0)

    def y_chip(i):
        return (ctx, x * NY + i)

    def project(h, i):
        cols = pl.ds(pl.multiple_of(i * FEAT, FEAT), FEAT)
        part = jnp.dot(att[h, 0], wall[0, :, cols], preferred_element_type=F32)
        for n in range(1, NX):
            part = part + jnp.dot(att[h, n], wall[n, :, cols], preferred_element_type=F32)
        return part

    def reduced(h, i, slot_there, to):
        return send(r_send.at[h, i], r_recv.at[h, slot_there], r_ss.at[h, i], r_rs.at[h, slot_there], to)

    for h in range(2):
        for d in (1, 2, 3):
            arrived(att.at[h, x_at[d]], a_rs.at[h, NX - d])
            if h == 0:
                arrived(wall.at[x_at[d], other], ws_rs.at[d])
        far_out[h] = project(h, far)

        @pl.when(at_end)
        def _():
            r_send[h, 0] = far_out[h].astype(BF16)
            reduced(h, 0, 3, y_chip(near))

        r_send[h, 1] = project(h, middle).astype(BF16)
        sent.append(reduced(h, 1, jnp.where(at_end, 0, 2), y_chip(middle)))
        r_send[h, 2] = project(h, near).astype(BF16)
        sent.append(reduced(h, 2, 1, y_chip(near)))
    for h in range(2):
        rows = slice(h * HALF, (h + 1) * HALF)
        own_out[rows] = project(h, y)

        @pl.when(jnp.logical_not(at_end))
        def _():
            arrived(r_recv.at[h, 3], r_rs.at[h, 3])
            r_send[h, 0] = (far_out[h] + r_recv[h, 3].astype(F32)).astype(BF16)
            reduced(h, 0, 0, y_chip(far))

    for h in range(2):
        rows = slice(h * HALF, (h + 1) * HALF)
        arrived(r_send.at[h, 0], r_ss.at[h, 0])

        @pl.when(jnp.logical_not(at_end))
        def _():
            arrived(r_recv.at[h, 2], r_rs.at[h, 2])
            own_out[rows] = own_out[rows] + r_recv[h, 2].astype(F32)

        for i in range(2):
            arrived(r_recv.at[h, i], r_rs.at[h, i])
        out_ref[rows] = (
            own_out[rows] + r_recv[h, 0].astype(F32) + r_recv[h, 1].astype(F32)
        ).astype(BF16)
    for copy in sent:
        copy.wait_send()


def local(
    queries, incoming_keys, incoming_values, cache_keys, stored_value_rows, cache_valid, out_weight
):
    flat = [
        a.reshape(a.shape[0] * a.shape[1], a.shape[2])
        for a in (queries, incoming_keys, incoming_values, cache_keys, stored_value_rows)
    ]
    hbm = pl.BlockSpec(memory_space=pltpu.HBM)
    vmem = pltpu.VMEM
    dma = pltpu.SemaphoreType.DMA
    return pl.pallas_call(
        kernel,
        name="attend_project",
        out_shape=jax.ShapeDtypeStruct((TOK, FEAT), BF16),
        in_specs=[pl.BlockSpec(memory_space=pltpu.SMEM)] + [hbm] * 6,
        out_specs=pl.BlockSpec(memory_space=pltpu.VMEM),
        scratch_shapes=[
            vmem((2 * TOK, HEAD), BF16),
            vmem((CQ * NX, HEAD), BF16),
            vmem((CQ * NX, HEAD), BF16),
            vmem((TQ * NX, HEAD), BF16),
            vmem((TQ * NX, HEAD), BF16),
            vmem((NY, 2 * TOK, HEAD), BF16),
            vmem((NZ, NS, ROWS, HEAD), BF16),
            vmem((NS * KEYS, 2 * TOK), F32),
            vmem((NY, 1, 2 * TOK), F32),
            vmem((NY, 1, 2 * TOK), F32),
            vmem((NY, HEAD, 2 * TOK), F32),
            vmem((2, NY, HEAD + 16, TOK), BF16),
            vmem((2, NY, HEAD + 16, TOK), BF16),
            vmem((2, NX, HALF, 2 * HEAD), BF16),
            vmem((NX, 2 * HEAD, SPAN), BF16),
            vmem((2, NY - 1, HALF, FEAT), BF16),
            vmem((2, NY, HALF, FEAT), BF16),
            vmem((2, HALF, FEAT), F32),
            vmem((TOK, FEAT), F32),
            dma((6,)),
            dma((4,)), dma((4,)),
            dma((2, 2, 5)), dma((2, 2, 5)),
            dma((2, 8)), dma((2, 8)),
            dma((2, 4)), dma((2, 4)),
            dma((4,)), dma((4,)),
            dma((4,)), dma((4,)),
            dma((2, 4)), dma((2, 4)),
            dma((2, 3)), dma((2, 4)),
        ],
        compiler_params=pltpu.CompilerParams(
            collective_id=0, has_side_effects=True, vmem_limit_bytes=VMEM_LIMIT
        ),
        cost_estimate=pl.CostEstimate(
            flops=2_200_000_000, bytes_accessed=6_000_000, transcendentals=3_200_000
        ),
    )(cache_valid, *flat, out_weight)


def solution(mesh):
    placed = (
        P("ctx", "tp", None),
        P("ctx", None, None),
        P("ctx", None, None),
        P("ctx", None, None),
        P("ctx", None, None),
        P("ctx"),
        P("tp", None),
    )
    return jax.shard_map(
        local, mesh=mesh, in_specs=placed, out_specs=P("ctx", "tp"), check_vma=False
    )
```

```python
import jax
import jax.numpy as jnp
from jax import lax
from jax.experimental import pallas as pl
from jax.experimental.pallas import tpu as pltpu
from jax.sharding import PartitionSpec as P

MESH = pl.DeviceIdType.MESH
F32 = jnp.float32
BF16 = jnp.bfloat16

NX = 4
NY = 4
NZ = 8
NS = 4
HEAD = 128
TOK = 128
HALF = TOK // 2
CACHE = 256
CQ = CACHE // NY
TQ = TOK // NY
KEYS = CQ + TQ
ROWS = 2 * KEYS
DEAD = 64.0
FEAT = 512
SPAN = NY * FEAT
MASKED = -1e30
VMEM_LIMIT = 40 * 2**20
SCALE = HEAD ** (-0.5) * 1.4426950408889634


def nt(a, b):
    return lax.dot_general(a, b, (((1,), (1,)), ((), ())), preferred_element_type=F32)


def tn(a, b):
    return lax.dot_general(a, b, (((0,), (0,)), ((), ())), preferred_element_type=F32)


def pick(rows, wide, step, first):
    r = lax.broadcasted_iota(jnp.int32, (rows, wide), 0)
    c = lax.broadcasted_iota(jnp.int32, (rows, wide), 1)
    return jnp.where(c == step * r + first, 1.0, 0.0).astype(BF16)


def kernel(
    valid_ref, q_hbm, ik_hbm, iv_hbm, ck_hbm, cv_hbm, w_hbm, out_ref,
    q_raw, ck_raw, cv_raw, ik_raw, iv_raw,
    q_all, kv, bias, m_ref, l_ref, acc,
    o_send, o_recv,
    att, wall, r_send, r_recv, far_out, own_out,
    local_sem, q_ss, q_rs, kv_ss, kv_rs, sib_ss, sib_rs, o_ss, o_rs,
    w_ss, w_rs, ws_ss, ws_rs, a_ss, a_rs, r_ss, r_rs,
):
    ctx = lax.axis_index("ctx")
    tp = lax.axis_index("tp")
    x, y = tp // NY, tp % NY
    z, shard = ctx // NS, ctx % NS
    y_hi, core = shard // 2, shard % 2
    quarter = y_hi * (NY - 1 - y) + (1 - y_hi) * y
    z_peer = {k: (lax.rem(z + k + NZ, NZ) * NS + shard, tp) for k in (-2, -1, 1, 2)}
    sibling = (z * NS + y_hi * 2 + (1 - core), tp)
    mirror = (z * NS + (1 - y_hi) * 2 + core, x * NY + (NY - 1 - y))
    y_at = [lax.rem(y + d, NY) for d in range(NY)]
    x_at = [lax.rem(x + d, NX) for d in range(NX)]
    y_peer = [(ctx, x * NY + y_at[d]) for d in range(NY)]
    x_peer = [(ctx, x_at[d] * NY + y) for d in range(NX)]

    def send(src, dst, ss, rs, to):
        copy = pltpu.make_async_remote_copy(
            src_ref=src, dst_ref=dst, send_sem=ss, recv_sem=rs, device_id=to, device_id_type=MESH
        )
        copy.start()
        return copy

    def fetch(src, dst, sem):
        copy = pltpu.make_async_copy(src, dst, sem)
        copy.start()
        return copy

    sent = []

    barrier = pltpu.get_barrier_semaphore()
    partners = list(z_peer.values()) + [sibling, mirror] + y_peer[1:] + x_peer[1:]
    for partner in partners:
        pl.semaphore_signal(barrier, inc=1, device_id=partner, device_id_type=MESH)

    c_at = pl.multiple_of(quarter * (CQ * NX), CQ * NX)
    t_at = pl.multiple_of(quarter * (TQ * NX), TQ * NX)
    loads = [
        fetch(ck_hbm.at[pl.ds(c_at, CQ * NX)], ck_raw, local_sem.at[0]),
        fetch(ik_hbm.at[pl.ds(t_at, TQ * NX)], ik_raw, local_sem.at[1]),
        fetch(cv_hbm.at[pl.ds(c_at, CQ * NX)], cv_raw, local_sem.at[2]),
        fetch(iv_hbm.at[pl.ds(t_at, TQ * NX)], iv_raw, local_sem.at[3]),
        fetch(q_hbm, q_raw, local_sem.at[4]),
    ]

    take_c = pick(CQ, CQ * NX, NX, x)
    take_t = pick(TQ, TQ * NX, NX, x)
    own = kv.at[z, shard]
    loads[0].wait()
    slot_at = lax.broadcasted_iota(jnp.int32, (CQ, HEAD), 0) + quarter * CQ
    own[0:CQ] = jnp.where(
        slot_at < valid_ref[0], jnp.dot(take_c, ck_raw[...], preferred_element_type=F32), DEAD
    ).astype(BF16)
    loads[1].wait()
    own[CQ:KEYS] = jnp.dot(take_t, ik_raw[...], preferred_element_type=F32).astype(BF16)
    loads[2].wait()
    own[KEYS:KEYS + CQ] = jnp.dot(take_c, cv_raw[...], preferred_element_type=F32).astype(BF16)
    loads[3].wait()
    own[KEYS + CQ:ROWS] = jnp.dot(take_t, iv_raw[...], preferred_element_type=F32).astype(BF16)
    pl.semaphore_wait(barrier, len(partners))

    types = [shard, (1 - y_hi) * 2 + core]
    sib_types = [y_hi * 2 + (1 - core), (1 - y_hi) * 2 + (1 - core)]

    def slot(k):
        return lax.rem(z + k + NZ, NZ)

    def arrived(ref, sem):
        pltpu.make_async_copy(ref, ref, sem).wait()

    def ship(kind, k, hop):
        at = kv.at[slot(k), types[kind]]
        i = (k - hop) % NZ
        sent.append(send(at, at, kv_ss.at[kind, i], kv_rs.at[kind, i], z_peer[hop]))

    def spread(kind):
        for hop in (2, -2, 1, -1):
            ship(kind, 0, hop)

    def to_sibling(kind, k):
        at = kv.at[slot(k), types[kind]]
        i = k % NZ
        sent.append(send(at, at, sib_ss.at[kind, i], sib_rs.at[kind, i], sibling))

    def from_sibling(k):
        for kind in range(2):
            arrived(kv.at[slot(k), sib_types[kind]], sib_rs.at[kind, k % NZ])

    def take(kind, k):
        arrived(kv.at[slot(k), types[kind]], kv_rs.at[kind, k % NZ])
        if abs(k) == 2:
            onward = 1 if k < 0 else -1
            if k == (-2 if kind == 0 else 2):
                ship(kind, k, 2 * onward)
            ship(kind, k, onward)
        to_sibling(kind, k)

    sent.append(send(own, own, kv_ss.at[0, 0], kv_rs.at[0, 0], mirror))
    spread(0)
    to_sibling(0, 0)
    loads[4].wait()
    for i in range(4):
        q_all[0, i * HALF:(i + 1) * HALF] = jnp.dot(
            pick(HALF, 2 * TOK, 2, (i // 2) * TOK + i % 2), q_raw[...], preferred_element_type=F32
        ).astype(BF16)
    for d in (2, 1, 3):
        sent.append(send(q_all.at[0], q_all.at[NY - d], q_ss.at[d], q_rs.at[NY - d], y_peer[d]))

    half = pl.ds(pl.multiple_of(core * TOK, TOK), TOK)
    for d in (2, 1, 3):
        sent.append(
            send(
                w_hbm.at[half, pl.ds(pl.multiple_of(x_at[d] * SPAN, SPAN), SPAN)],
                wall.at[x, half],
                w_ss.at[d],
                w_rs.at[d],
                x_peer[d],
            )
        )
    w_own = fetch(
        w_hbm.at[:, pl.ds(pl.multiple_of(x * SPAN, SPAN), SPAN)], wall.at[x], local_sem.at[5]
    )

    lane = lax.broadcasted_iota(jnp.int32, (TQ, 2 * TOK), 1)
    token = lane // TOK * HALF + lane % HALF + ctx * TOK
    new_at = lax.broadcasted_iota(jnp.int32, (TQ, 2 * TOK), 0) + quarter * TQ

    def absorb(k, rows=range(NY), first=False, masks=True):
        zs = slot(k)
        if masks:
            for s in range(NS):
                b = jnp.where(kv[zs, s, 0:CQ].astype(F32) == DEAD, MASKED, 0.0)
                bias[s * KEYS:s * KEYS + CQ] = jnp.concatenate([b, b], axis=1)
                bias[s * KEYS + CQ:(s + 1) * KEYS] = jnp.where(
                    new_at + (zs * NS + s) * TOK <= token, 0.0, MASKED
                )
        keys = jnp.concatenate([kv[zs, s, 0:KEYS] for s in range(NS)], axis=0)
        values = jnp.concatenate([kv[zs, s, KEYS:ROWS] for s in range(NS)], axis=0)

        def scored(j):
            return nt(keys, q_all[j]) * SCALE + bias[...]

        ready = scored(rows[0])
        for j in rows:
            scores = ready
            if j != rows[-1]:
                ready = scored(j + 1)
            top = jnp.max(scores, axis=0, keepdims=True)
            if first:
                weights = jnp.exp2(scores - top)
                m_ref[j] = top
                l_ref[j] = jnp.sum(weights, axis=0, keepdims=True)
                acc[j] = tn(values, weights.astype(BF16))
            else:
                old = m_ref[j]
                new = jnp.maximum(old, top)
                rescale = jnp.exp2(old - new)
                weights = jnp.exp2(scores - new)
                m_ref[j] = new
                l_ref[j] = l_ref[j] * rescale + jnp.sum(weights, axis=0, keepdims=True)
                acc[j] = acc[j] * rescale + tn(values, weights.astype(BF16))

    arrived(kv.at[z, types[1]], kv_rs.at[0, 0])
    spread(1)
    to_sibling(1, 0)
    take(0, 2)
    take(0, -2)
    take(0, 1)
    take(0, -1)
    take(1, 2)
    take(1, -2)
    from_sibling(0)
    absorb(0, range(1), first=True)
    take(1, 1)
    take(1, -1)
    for d in (1, 2, 3):
        arrived(q_all.at[d], q_rs.at[d])
    absorb(0, range(1, NY), first=True, masks=False)
    from_sibling(2)
    absorb(2)
    take(0, 4)
    from_sibling(-2)
    absorb(-2)
    take(0, 3)
    take(0, -3)
    from_sibling(1)
    absorb(1)
    take(1, 4)
    from_sibling(-1)
    absorb(-1)
    take(1, 3)
    take(1, -3)
    for k in (4, 3, -3):
        from_sibling(k)
        absorb(k)

    def parts(e):
        row = lax.broadcasted_iota(jnp.int32, (16, TOK), 0)
        high = e.astype(BF16).astype(F32)
        middle = (e - high).astype(BF16).astype(F32)
        return jnp.where(row == 0, high, jnp.where(row == 1, middle, e - high - middle)).astype(BF16)

    own_lse = [None, None]
    for h in range(2):
        lanes = slice(h * TOK, (h + 1) * TOK)
        for d in (2, 1, 3, 0):
            total = l_ref[d, :, lanes]
            o_send[h, d, 0:HEAD] = (acc[d, :, lanes] / total).astype(BF16)
            e = m_ref[d, :, lanes] + jnp.log2(total)
            if d:
                o_send[h, d, HEAD:] = parts(e)
                sent.append(send(o_send.at[h, d], o_recv.at[h, d], o_ss.at[h, d], o_rs.at[h, d], y_peer[d]))
            else:
                own_lse[h] = e
    for d in (1, 2, 3):
        at = wall.at[x_at[d], half]
        arrived(at, w_rs.at[NX - d])
        sent.append(send(at, at, ws_ss.at[d], ws_rs.at[d], sibling))
    for h in range(2):
        lse = [own_lse[h]]
        for d in (1, 2, 3):
            arrived(o_recv.at[h, d], o_rs.at[h, d])
            e = o_recv[h, d, HEAD:].astype(F32)
            lse.append(e[0:1] + e[1:2] + e[2:3])
        top = jnp.maximum(jnp.maximum(lse[0], lse[1]), jnp.maximum(lse[2], lse[3]))
        share = [jnp.exp2(e - top) for e in lse]
        whole = share[0] + share[1] + share[2] + share[3]
        mixed = o_send[h, 0, 0:HEAD].astype(F32) * (share[0] / whole)
        for d in (1, 2, 3):
            mixed = mixed + o_recv[h, d, 0:HEAD].astype(F32) * (share[d] / whole)
        turned = mixed.T.astype(BF16)
        att[h, x, :, 0:HEAD] = turned[0:HALF]
        att[h, x, :, HEAD:2 * HEAD] = turned[HALF:TOK]
        a_own = att.at[h, x]
        for d in (2, 1, 3):
            sent.append(send(a_own, a_own, a_ss.at[h, d], a_rs.at[h, d], x_peer[d]))
    w_own.wait()
    other = pl.ds(pl.multiple_of((1 - core) * TOK, TOK), TOK)

    at_end = jnp.logical_or(y == 0, y == NY - 1)
    near = y + 1 - 2 * lax.rem(y, 2)
    middle = jnp.where(y < 2, 2, 1)
    far = jnp.where(y < 2, 3, 0)

    def y_chip(i):
        return (ctx, x * NY + i)

    def project(h, i):
        cols = pl.ds(pl.multiple_of(i * FEAT, FEAT), FEAT)
        part = jnp.dot(att[h, 0], wall[0, :, cols], preferred_element_type=F32)
        for n in range(1, NX):
            part = part + jnp.dot(att[h, n], wall[n, :, cols], preferred_element_type=F32)
        return part

    def reduced(h, i, slot_there, to):
        return send(r_send.at[h, i], r_recv.at[h, slot_there], r_ss.at[h, i], r_rs.at[h, slot_there], to)

    for h in range(2):
        for d in (1, 2, 3):
            arrived(att.at[h, x_at[d]], a_rs.at[h, NX - d])
            if h == 0:
                arrived(wall.at[x_at[d], other], ws_rs.at[d])
        far_out[h] = project(h, far)

        @pl.when(at_end)
        def _():
            r_send[h, 0] = far_out[h].astype(BF16)
            reduced(h, 0, 3, y_chip(near))

        r_send[h, 1] = project(h, middle).astype(BF16)
        sent.append(reduced(h, 1, jnp.where(at_end, 0, 2), y_chip(middle)))
        r_send[h, 2] = project(h, near).astype(BF16)
        sent.append(reduced(h, 2, 1, y_chip(near)))
    for h in range(2):
        rows = slice(h * HALF, (h + 1) * HALF)
        own_out[rows] = project(h, y)

        @pl.when(jnp.logical_not(at_end))
        def _():
            arrived(r_recv.at[h, 3], r_rs.at[h, 3])
            r_send[h, 0] = (far_out[h] + r_recv[h, 3].astype(F32)).astype(BF16)
            reduced(h, 0, 0, y_chip(far))

    for h in range(2):
        rows = slice(h * HALF, (h + 1) * HALF)
        arrived(r_send.at[h, 0], r_ss.at[h, 0])

        @pl.when(jnp.logical_not(at_end))
        def _():
            arrived(r_recv.at[h, 2], r_rs.at[h, 2])
            own_out[rows] = own_out[rows] + r_recv[h, 2].astype(F32)

        for i in range(2):
            arrived(r_recv.at[h, i], r_rs.at[h, i])
        out_ref[rows] = (
            own_out[rows] + r_recv[h, 0].astype(F32) + r_recv[h, 1].astype(F32)
        ).astype(BF16)
    for copy in sent:
        copy.wait_send()


def local(
    queries, incoming_keys, incoming_values, cache_keys, stored_value_rows, cache_valid, out_weight
):
    flat = [
        a.reshape(a.shape[0] * a.shape[1], a.shape[2])
        for a in (queries, incoming_keys, incoming_values, cache_keys, stored_value_rows)
    ]
    hbm = pl.BlockSpec(memory_space=pltpu.HBM)
    vmem = pltpu.VMEM
    dma = pltpu.SemaphoreType.DMA
    return pl.pallas_call(
        kernel,
        name="attend_project",
        out_shape=jax.ShapeDtypeStruct((TOK, FEAT), BF16),
        in_specs=[pl.BlockSpec(memory_space=pltpu.SMEM)] + [hbm] * 6,
        out_specs=pl.BlockSpec(memory_space=pltpu.VMEM),
        scratch_shapes=[
            vmem((2 * TOK, HEAD), BF16),
            vmem((CQ * NX, HEAD), BF16),
            vmem((CQ * NX, HEAD), BF16),
            vmem((TQ * NX, HEAD), BF16),
            vmem((TQ * NX, HEAD), BF16),
            vmem((NY, 2 * TOK, HEAD), BF16),
            vmem((NZ, NS, ROWS, HEAD), BF16),
            vmem((NS * KEYS, 2 * TOK), F32),
            vmem((NY, 1, 2 * TOK), F32),
            vmem((NY, 1, 2 * TOK), F32),
            vmem((NY, HEAD, 2 * TOK), F32),
            vmem((2, NY, HEAD + 16, TOK), BF16),
            vmem((2, NY, HEAD + 16, TOK), BF16),
            vmem((2, NX, HALF, 2 * HEAD), BF16),
            vmem((NX, 2 * HEAD, SPAN), BF16),
            vmem((2, NY - 1, HALF, FEAT), BF16),
            vmem((2, NY, HALF, FEAT), BF16),
            vmem((2, HALF, FEAT), F32),
            vmem((TOK, FEAT), F32),
            dma((6,)),
            dma((4,)), dma((4,)),
            dma((2, 8)), dma((2, 8)),
            dma((2, 8)), dma((2, 8)),
            dma((2, 4)), dma((2, 4)),
            dma((4,)), dma((4,)),
            dma((4,)), dma((4,)),
            dma((2, 4)), dma((2, 4)),
            dma((2, 3)), dma((2, 4)),
        ],
        compiler_params=pltpu.CompilerParams(
            collective_id=0, has_side_effects=True, vmem_limit_bytes=VMEM_LIMIT
        ),
        cost_estimate=pl.CostEstimate(
            flops=2_200_000_000, bytes_accessed=6_000_000, transcendentals=3_200_000
        ),
    )(cache_valid, *[pltpu.with_memory_space_constraint(a, pltpu.HBM) for a in flat + [out_weight]])


def solution(mesh):
    placed = (
        P("ctx", "tp", None),
        P("ctx", None, None),
        P("ctx", None, None),
        P("ctx", None, None),
        P("ctx", None, None),
        P("ctx"),
        P("tp", None),
    )
    return jax.shard_map(
        local, mesh=mesh, in_specs=placed, out_specs=P("ctx", "tp"), check_vma=False
    )
```

```python
import jax
import jax.numpy as jnp
from jax import lax
from jax.experimental import pallas as pl
from jax.experimental.pallas import tpu as pltpu
from jax.sharding import PartitionSpec as P

MESH = pl.DeviceIdType.MESH
F32 = jnp.float32
BF16 = jnp.bfloat16

NX = 4
NY = 4
NZ = 8
NS = 4
HEAD = 128
TOK = 128
HALF = TOK // 2
CACHE = 256
CQ = CACHE // NY
TQ = TOK // NY
KEYS = CQ + TQ
ROWS = 2 * KEYS
DEAD = 64.0
FEAT = 512
SPAN = NY * FEAT
MASKED = -1e30
VMEM_LIMIT = 40 * 2**20
SCALE = HEAD ** (-0.5) * 1.4426950408889634


def nt(a, b):
    return lax.dot_general(a, b, (((1,), (1,)), ((), ())), preferred_element_type=F32)


def tn(a, b):
    return lax.dot_general(a, b, (((0,), (0,)), ((), ())), preferred_element_type=F32)


def pick(rows, wide, step, first):
    r = lax.broadcasted_iota(jnp.int32, (rows, wide), 0)
    c = lax.broadcasted_iota(jnp.int32, (rows, wide), 1)
    return jnp.where(c == step * r + first, 1.0, 0.0).astype(BF16)


def kernel(
    valid_ref, q_hbm, ik_hbm, iv_hbm, ck_hbm, cv_hbm, w_hbm, out_ref,
    q_raw, ck_raw, cv_raw, ik_raw, iv_raw,
    q_all, kv, bias, m_ref, l_ref, acc,
    o_send, o_recv,
    att, wall, r_send, r_recv, far_out, own_out,
    local_sem, q_ss, q_rs, kv_ss, kv_rs, sib_ss, sib_rs, o_ss, o_rs,
    w_ss, w_rs, ws_ss, ws_rs, a_ss, a_rs, r_ss, r_rs,
):
    ctx = lax.axis_index("ctx")
    tp = lax.axis_index("tp")
    x, y = tp // NY, tp % NY
    z, shard = ctx // NS, ctx % NS
    y_hi, core = shard // 2, shard % 2
    quarter = y_hi * (NY - 1 - y) + (1 - y_hi) * y
    z_peer = {k: (lax.rem(z + k + NZ, NZ) * NS + shard, tp) for k in (-2, -1, 1, 2)}
    sibling = (z * NS + y_hi * 2 + (1 - core), tp)
    mirror = (z * NS + (1 - y_hi) * 2 + core, x * NY + (NY - 1 - y))
    y_at = [lax.rem(y + d, NY) for d in range(NY)]
    x_at = [lax.rem(x + d, NX) for d in range(NX)]
    y_peer = [(ctx, x * NY + y_at[d]) for d in range(NY)]
    x_peer = [(ctx, x_at[d] * NY + y) for d in range(NX)]

    def send(src, dst, ss, rs, to):
        copy = pltpu.make_async_remote_copy(
            src_ref=src, dst_ref=dst, send_sem=ss, recv_sem=rs, device_id=to, device_id_type=MESH
        )
        copy.start()
        return copy

    def fetch(src, dst, sem):
        copy = pltpu.make_async_copy(src, dst, sem)
        copy.start()
        return copy

    sent = []

    barrier = pltpu.get_barrier_semaphore()
    partners = list(z_peer.values()) + [sibling, mirror] + y_peer[1:] + x_peer[1:]
    for partner in partners:
        pl.semaphore_signal(barrier, inc=1, device_id=partner, device_id_type=MESH)

    c_at = pl.multiple_of(quarter * (CQ * NX), CQ * NX)
    t_at = pl.multiple_of(quarter * (TQ * NX), TQ * NX)
    loads = [
        fetch(ck_hbm.at[pl.ds(c_at, CQ * NX)], ck_raw, local_sem.at[0]),
        fetch(ik_hbm.at[pl.ds(t_at, TQ * NX)], ik_raw, local_sem.at[1]),
        fetch(cv_hbm.at[pl.ds(c_at, CQ * NX)], cv_raw, local_sem.at[2]),
        fetch(iv_hbm.at[pl.ds(t_at, TQ * NX)], iv_raw, local_sem.at[3]),
        fetch(q_hbm, q_raw, local_sem.at[4]),
    ]

    take_c = pick(CQ, CQ * NX, NX, x)
    take_t = pick(TQ, TQ * NX, NX, x)
    own = kv.at[z, shard]
    loads[0].wait()
    slot_at = lax.broadcasted_iota(jnp.int32, (CQ, HEAD), 0) + quarter * CQ
    own[0:CQ] = jnp.where(
        slot_at < valid_ref[0], jnp.dot(take_c, ck_raw[...], preferred_element_type=F32), DEAD
    ).astype(BF16)
    loads[1].wait()
    own[CQ:KEYS] = jnp.dot(take_t, ik_raw[...], preferred_element_type=F32).astype(BF16)
    loads[2].wait()
    own[KEYS:KEYS + CQ] = jnp.dot(take_c, cv_raw[...], preferred_element_type=F32).astype(BF16)
    loads[3].wait()
    own[KEYS + CQ:ROWS] = jnp.dot(take_t, iv_raw[...], preferred_element_type=F32).astype(BF16)
    pl.semaphore_wait(barrier, len(partners))

    types = [shard, (1 - y_hi) * 2 + core]
    sib_types = [y_hi * 2 + (1 - core), (1 - y_hi) * 2 + (1 - core)]

    def slot(k):
        return lax.rem(z + k + NZ, NZ)

    def arrived(ref, sem):
        pltpu.make_async_copy(ref, ref, sem).wait()

    def ship(kind, k, hop):
        at = kv.at[slot(k), types[kind]]
        i = (k - hop) % NZ
        sent.append(send(at, at, kv_ss.at[kind, i], kv_rs.at[kind, i], z_peer[hop]))

    def spread(kind):
        for hop in (2, -2, 1, -1):
            ship(kind, 0, hop)

    def to_sibling(kind, k):
        at = kv.at[slot(k), types[kind]]
        i = k % NZ
        sent.append(send(at, at, sib_ss.at[kind, i], sib_rs.at[kind, i], sibling))

    def from_sibling(k):
        for kind in range(2):
            arrived(kv.at[slot(k), sib_types[kind]], sib_rs.at[kind, k % NZ])

    def take(kind, k):
        arrived(kv.at[slot(k), types[kind]], kv_rs.at[kind, k % NZ])
        if abs(k) == 2:
            onward = 1 if k < 0 else -1
            if k == (-2 if kind == 0 else 2):
                ship(kind, k, 2 * onward)
            ship(kind, k, onward)
        to_sibling(kind, k)

    sent.append(send(own, own, kv_ss.at[0, 0], kv_rs.at[0, 0], mirror))
    spread(0)
    to_sibling(0, 0)
    loads[4].wait()
    for i in range(4):
        q_all[0, i * HALF:(i + 1) * HALF] = jnp.dot(
            pick(HALF, 2 * TOK, 2, (i // 2) * TOK + i % 2), q_raw[...], preferred_element_type=F32
        ).astype(BF16)
    for d in (2, 1, 3):
        sent.append(send(q_all.at[0], q_all.at[NY - d], q_ss.at[d], q_rs.at[NY - d], y_peer[d]))

    half = pl.ds(pl.multiple_of(core * TOK, TOK), TOK)
    odd = lax.rem(z, 2)
    mine = pl.ds(pl.multiple_of(core * TOK + odd * HALF, HALF), HALF)
    theirs = pl.ds(pl.multiple_of(core * TOK + (1 - odd) * HALF, HALF), HALF)
    z_pair = ((z + 1 - 2 * odd) * NS + shard, tp)
    for d in (2, 1, 3):
        rows = mine if d == 2 else half
        sent.append(
            send(
                w_hbm.at[rows, pl.ds(pl.multiple_of(x_at[d] * SPAN, SPAN), SPAN)],
                wall.at[x, rows],
                w_ss.at[d],
                w_rs.at[d],
                x_peer[d],
            )
        )
    w_own = fetch(
        w_hbm.at[:, pl.ds(pl.multiple_of(x * SPAN, SPAN), SPAN)], wall.at[x], local_sem.at[5]
    )

    lane = lax.broadcasted_iota(jnp.int32, (TQ, 2 * TOK), 1)
    token = lane // TOK * HALF + lane % HALF + ctx * TOK
    new_at = lax.broadcasted_iota(jnp.int32, (TQ, 2 * TOK), 0) + quarter * TQ

    def absorb(k, rows=range(NY), first=False, masks=True):
        zs = slot(k)
        if masks:
            for s in range(NS):
                b = jnp.where(kv[zs, s, 0:CQ].astype(F32) == DEAD, MASKED, 0.0)
                bias[s * KEYS:s * KEYS + CQ] = jnp.concatenate([b, b], axis=1)
                bias[s * KEYS + CQ:(s + 1) * KEYS] = jnp.where(
                    new_at + (zs * NS + s) * TOK <= token, 0.0, MASKED
                )
        keys = jnp.concatenate([kv[zs, s, 0:KEYS] for s in range(NS)], axis=0)
        values = jnp.concatenate([kv[zs, s, KEYS:ROWS] for s in range(NS)], axis=0)

        def scored(j):
            return nt(keys, q_all[j]) * SCALE + bias[...]

        ready = scored(rows[0])
        for j in rows:
            scores = ready
            if j != rows[-1]:
                ready = scored(j + 1)
            top = jnp.max(scores, axis=0, keepdims=True)
            if first:
                weights = jnp.exp2(scores - top)
                m_ref[j] = top
                l_ref[j] = jnp.sum(weights, axis=0, keepdims=True)
                acc[j] = tn(values, weights.astype(BF16))
            else:
                old = m_ref[j]
                new = jnp.maximum(old, top)
                rescale = jnp.exp2(old - new)
                weights = jnp.exp2(scores - new)
                m_ref[j] = new
                l_ref[j] = l_ref[j] * rescale + jnp.sum(weights, axis=0, keepdims=True)
                acc[j] = acc[j] * rescale + tn(values, weights.astype(BF16))

    arrived(kv.at[z, types[1]], kv_rs.at[0, 0])
    spread(1)
    to_sibling(1, 0)
    take(0, 2)
    take(0, -2)
    take(0, 1)
    take(0, -1)
    take(1, 2)
    take(1, -2)
    from_sibling(0)
    absorb(0, range(1), first=True)
    take(1, 1)
    take(1, -1)
    for d in (1, 2, 3):
        arrived(q_all.at[d], q_rs.at[d])
    absorb(0, range(1, NY), first=True, masks=False)
    take(0, 4)
    from_sibling(2)
    absorb(2)
    take(0, 3)
    take(0, -3)
    from_sibling(-2)
    absorb(-2)
    take(1, 4)
    from_sibling(1)
    absorb(1)
    take(1, 3)
    take(1, -3)
    from_sibling(-1)
    absorb(-1)
    at = wall.at[x_at[2], mine]
    arrived(at, w_rs.at[2])
    sent.append(send(at, at, ws_ss.at[0], ws_rs.at[0], z_pair))
    for k in (4, 3, -3):
        from_sibling(k)
        absorb(k)

    def parts(e):
        row = lax.broadcasted_iota(jnp.int32, (16, TOK), 0)
        high = e.astype(BF16).astype(F32)
        middle = (e - high).astype(BF16).astype(F32)
        return jnp.where(row == 0, high, jnp.where(row == 1, middle, e - high - middle)).astype(BF16)

    own_lse = [None, None]
    for h in range(2):
        lanes = slice(h * TOK, (h + 1) * TOK)
        for d in (2, 1, 3, 0):
            total = l_ref[d, :, lanes]
            o_send[h, d, 0:HEAD] = (acc[d, :, lanes] / total).astype(BF16)
            e = m_ref[d, :, lanes] + jnp.log2(total)
            if d:
                o_send[h, d, HEAD:] = parts(e)
                sent.append(send(o_send.at[h, d], o_recv.at[h, d], o_ss.at[h, d], o_rs.at[h, d], y_peer[d]))
            else:
                own_lse[h] = e
    for d in (1, 3, 2):
        at = wall.at[x_at[d], half]
        if d == 2:
            arrived(wall.at[x_at[d], theirs], ws_rs.at[0])
        else:
            arrived(at, w_rs.at[NX - d])
        sent.append(send(at, at, ws_ss.at[d], ws_rs.at[d], sibling))
    for h in range(2):
        lse = [own_lse[h]]
        for d in (1, 2, 3):
            arrived(o_recv.at[h, d], o_rs.at[h, d])
            e = o_recv[h, d, HEAD:].astype(F32)
            lse.append(e[0:1] + e[1:2] + e[2:3])
        top = jnp.maximum(jnp.maximum(lse[0], lse[1]), jnp.maximum(lse[2], lse[3]))
        share = [jnp.exp2(e - top) for e in lse]
        whole = share[0] + share[1] + share[2] + share[3]
        mixed = o_send[h, 0, 0:HEAD].astype(F32) * (share[0] / whole)
        for d in (1, 2, 3):
            mixed = mixed + o_recv[h, d, 0:HEAD].astype(F32) * (share[d] / whole)
        turned = mixed.T.astype(BF16)
        att[h, x, :, 0:HEAD] = turned[0:HALF]
        att[h, x, :, HEAD:2 * HEAD] = turned[HALF:TOK]
        a_own = att.at[h, x]
        for d in (2, 1, 3):
            sent.append(send(a_own, a_own, a_ss.at[h, d], a_rs.at[h, d], x_peer[d]))
    w_own.wait()
    other = pl.ds(pl.multiple_of((1 - core) * TOK, TOK), TOK)

    at_end = jnp.logical_or(y == 0, y == NY - 1)
    near = y + 1 - 2 * lax.rem(y, 2)
    middle = jnp.where(y < 2, 2, 1)
    far = jnp.where(y < 2, 3, 0)

    def y_chip(i):
        return (ctx, x * NY + i)

    def project(h, i):
        cols = pl.ds(pl.multiple_of(i * FEAT, FEAT), FEAT)
        part = jnp.dot(att[h, 0], wall[0, :, cols], preferred_element_type=F32)
        for n in range(1, NX):
            part = part + jnp.dot(att[h, n], wall[n, :, cols], preferred_element_type=F32)
        return part

    def reduced(h, i, slot_there, to):
        return send(r_send.at[h, i], r_recv.at[h, slot_there], r_ss.at[h, i], r_rs.at[h, slot_there], to)

    for h in range(2):
        for d in (1, 2, 3):
            arrived(att.at[h, x_at[d]], a_rs.at[h, NX - d])
            if h == 0:
                arrived(wall.at[x_at[d], other], ws_rs.at[d])
        far_out[h] = project(h, far)

        @pl.when(at_end)
        def _():
            r_send[h, 0] = far_out[h].astype(BF16)
            reduced(h, 0, 3, y_chip(near))

        r_send[h, 1] = project(h, middle).astype(BF16)
        sent.append(reduced(h, 1, jnp.where(at_end, 0, 2), y_chip(middle)))
        r_send[h, 2] = project(h, near).astype(BF16)
        sent.append(reduced(h, 2, 1, y_chip(near)))
    for h in range(2):
        rows = slice(h * HALF, (h + 1) * HALF)
        own_out[rows] = project(h, y)

        @pl.when(jnp.logical_not(at_end))
        def _():
            arrived(r_recv.at[h, 3], r_rs.at[h, 3])
            r_send[h, 0] = (far_out[h] + r_recv[h, 3].astype(F32)).astype(BF16)
            reduced(h, 0, 0, y_chip(far))

    for h in range(2):
        rows = slice(h * HALF, (h + 1) * HALF)
        arrived(r_send.at[h, 0], r_ss.at[h, 0])

        @pl.when(jnp.logical_not(at_end))
        def _():
            arrived(r_recv.at[h, 2], r_rs.at[h, 2])
            own_out[rows] = own_out[rows] + r_recv[h, 2].astype(F32)

        for i in range(2):
            arrived(r_recv.at[h, i], r_rs.at[h, i])
        out_ref[rows] = (
            own_out[rows] + r_recv[h, 0].astype(F32) + r_recv[h, 1].astype(F32)
        ).astype(BF16)
    for copy in sent:
        copy.wait_send()


def local(
    queries, incoming_keys, incoming_values, cache_keys, stored_value_rows, cache_valid, out_weight
):
    flat = [
        a.reshape(a.shape[0] * a.shape[1], a.shape[2])
        for a in (queries, incoming_keys, incoming_values, cache_keys, stored_value_rows)
    ]
    hbm = pl.BlockSpec(memory_space=pltpu.HBM)
    vmem = pltpu.VMEM
    dma = pltpu.SemaphoreType.DMA
    return pl.pallas_call(
        kernel,
        name="attend_project",
        out_shape=jax.ShapeDtypeStruct((TOK, FEAT), BF16),
        in_specs=[pl.BlockSpec(memory_space=pltpu.SMEM)] + [hbm] * 6,
        out_specs=pl.BlockSpec(memory_space=pltpu.VMEM),
        scratch_shapes=[
            vmem((2 * TOK, HEAD), BF16),
            vmem((CQ * NX, HEAD), BF16),
            vmem((CQ * NX, HEAD), BF16),
            vmem((TQ * NX, HEAD), BF16),
            vmem((TQ * NX, HEAD), BF16),
            vmem((NY, 2 * TOK, HEAD), BF16),
            vmem((NZ, NS, ROWS, HEAD), BF16),
            vmem((NS * KEYS, 2 * TOK), F32),
            vmem((NY, 1, 2 * TOK), F32),
            vmem((NY, 1, 2 * TOK), F32),
            vmem((NY, HEAD, 2 * TOK), F32),
            vmem((2, NY, HEAD + 16, TOK), BF16),
            vmem((2, NY, HEAD + 16, TOK), BF16),
            vmem((2, NX, HALF, 2 * HEAD), BF16),
            vmem((NX, 2 * HEAD, SPAN), BF16),
            vmem((2, NY - 1, HALF, FEAT), BF16),
            vmem((2, NY, HALF, FEAT), BF16),
            vmem((2, HALF, FEAT), F32),
            vmem((TOK, FEAT), F32),
            dma((6,)),
            dma((4,)), dma((4,)),
            dma((2, 8)), dma((2, 8)),
            dma((2, 8)), dma((2, 8)),
            dma((2, 4)), dma((2, 4)),
            dma((4,)), dma((4,)),
            dma((4,)), dma((4,)),
            dma((2, 4)), dma((2, 4)),
            dma((2, 3)), dma((2, 4)),
        ],
        compiler_params=pltpu.CompilerParams(
            collective_id=0, has_side_effects=True, vmem_limit_bytes=VMEM_LIMIT
        ),
        cost_estimate=pl.CostEstimate(
            flops=2_200_000_000, bytes_accessed=6_000_000, transcendentals=3_200_000
        ),
    )(cache_valid, *[pltpu.with_memory_space_constraint(a, pltpu.HBM) for a in flat + [out_weight]])


def solution(mesh):
    placed = (
        P("ctx", "tp", None),
        P("ctx", None, None),
        P("ctx", None, None),
        P("ctx", None, None),
        P("ctx", None, None),
        P("ctx"),
        P("tp", None),
    )
    return jax.shard_map(
        local, mesh=mesh, in_specs=placed, out_specs=P("ctx", "tp"), check_vma=False
    )
```
